32 devices in a mesh: space: 4 (over y, core), tm: 8 (over z, x).
Axes of the slice: x: 2, y: 2, z: 4, core: 2. Of those that a mesh axis runs over, the one named last changes fastest.
Arguments:
- space_factor: bfloat16 [64, 16384], P('tm', 'space'), may hold values from -2.5 to 2.5
- time_factor: bfloat16 [64, 2048], P('space', 'tm'), may hold values from -2.5 to 2.5
- initial_state: float32 [16384], P('space'), may hold values from -6 to 6
- link: int32 [16384], P('space'), may hold values from 1 to 4
- conductivity: float32 [16384], P('space'), may hold values from 0.2 to 2
- mass: float32 [16384], P('space'), may hold values from 0.5 to 2
- reaction: float32 [16384], P('space'), may hold values from 0.05 to 0.4
- source: bfloat16 [16384, 2048], P('space', 'tm'), may hold values from -6 to 6
Outputs:
- grad_space: float32 [64, 16384], P('tm', 'space')
- grad_time: float32 [64, 2048], P('space', 'tm')
The draws below stay inside these ranges and needn't reach their ends.
Inputs may be any that keep to these rules, and one draw needn't show every extreme that they name: Element i joins node i and node i + link[i]; where that node lies past the last node, the element ties node i to a zero value.
All inputs are finite; a program needn't handle non-finite values.
Results may differ from the reference program's by a relative error of at most 0.00055.
Values may be sent and summed in bfloat16 or wider, within the bound.
A program may use at most 64 MiB of HBM per device.

```python
import math
import jax
import jax.numpy as jnp
from jax import lax

R = 64
W = 4
STEP_DEV = 256
NODES = 16384
STEPS = 2048
N_TM = 8


def plant(values, key, low, largest):
    spot = [jax.random.randint(jax.random.fold_in(key, axis), (), 0, length) for axis, length in enumerate(values.shape)]
    widest = values.shape.index(max(values.shape))
    neighbour = spot[:widest] + [(spot[widest] + 1) % values.shape[widest]] + spot[widest + 1:]
    return values.at[tuple(spot)].set(low).at[tuple(neighbour)].set(largest)


def block_levels(own_key, extent, cuts, least, high):
    gain = 1.0
    for axis_at, parts in cuts:
        steps = jax.random.uniform(jax.random.fold_in(jax.random.fold_in(own_key, 6), axis_at), (parts,), jnp.float32, least / len(cuts), high / len(cuts))
        gain = gain * jnp.repeat(jnp.exp(steps), extent[axis_at] // parts).reshape((-1,) + (1,) * (len(extent) - 1 - axis_at))
    return gain


def gaussian(own_key, extent, width, limit, cuts=(), kind=jnp.bfloat16):
    array = jax.random.normal(own_key, extent, jnp.float32) * width
    if len(cuts) > 0:
        array = block_levels(own_key, extent, cuts, -0.22, 0.18) * array
    return jnp.clip(array, min=-limit, max=limit).astype(kind)


def setup_inputs(seed: int = 0) -> dict:
    arg_keys = jax.random.split(jax.random.key(seed), 9)
    space_factor = gaussian(arg_keys[0], (R, NODES), 0.35, 2.5, ((0, 8), (1, 4)))
    time_factor = gaussian(arg_keys[1], (R, STEPS), 0.35, 2.5, ((0, 4), (1, 8)))
    initial_state = gaussian(arg_keys[2], (NODES,), 1.0, 6.0, ((0, 4),), jnp.float32)
    link = plant(jax.random.randint(arg_keys[3], (NODES,), 1, W + 1), jax.random.fold_in(arg_keys[3], 1), 1, W).astype(jnp.int32)
    conductivity = jnp.clip(jnp.exp(math.log(2.0) - 2.3025851 * jax.random.uniform(arg_keys[4], (NODES,), jnp.float32) ** block_levels(arg_keys[4], (NODES,), ((0, 4),), -0.2, 0.2)), 0.2, 2.0)
    mass = jnp.clip(jnp.exp(math.log(2.0) - 1.3862944 * jax.random.uniform(arg_keys[5], (NODES,), jnp.float32) ** block_levels(arg_keys[5], (NODES,), ((0, 4),), -0.2, 0.2)), 0.5, 2.0)
    reaction = jnp.clip(jnp.exp(math.log(0.4) - 2.0794415 * jax.random.uniform(arg_keys[6], (NODES,), jnp.float32) ** block_levels(arg_keys[6], (NODES,), ((0, 4),), -0.2, 0.2)), 0.05, 0.4)
    source = gaussian(arg_keys[7], (NODES, STEPS), 1.0, 6.0, ((0, 4), (1, 8)))
    return dict(space_factor=space_factor, time_factor=time_factor, initial_state=initial_state, link=link, conductivity=conductivity, mass=mass, reaction=reaction, source=source)


def diffuse(padded, rates_padded, count):
    total = None
    for offset in range(1, W + 1):
        own_rate = rates_padded[offset - 1, W:W + count][:, None]
        came_rate = rates_padded[offset - 1, W - offset:W - offset + count][:, None]
        centre = padded[W:W + count]
        term = own_rate * (centre - padded[W + offset:W + offset + count]) - came_rate * (padded[W - offset:W - offset + count] - centre)
        total = term if total is None else total + term
    return total

def reference(space_factor, time_factor, initial_state, link, conductivity, mass, reaction, source):
    offsets = jnp.arange(1, W + 1, dtype=jnp.int32)[:, None]
    rates = jnp.where(link[None, :] == offsets, conductivity[None, :], 0.0)
    rates_padded = jnp.pad(rates, ((0, 0), (W, W)))
    zero_col = jnp.zeros((R, 1), time_factor.dtype)
    time_padded = jnp.concatenate([zero_col, time_factor, zero_col], axis=1)
    source_padded = jnp.concatenate([source, jnp.zeros((NODES, 1), source.dtype)], axis=1)
    space_t = space_factor.T
    mass_col = mass[:, None]
    react_col = reaction[:, None]

    def advance(accum, block):
        begin = block * STEP_DEV
        window = lax.dynamic_slice_in_dim(time_padded, begin, STEP_DEV + 2, 1)
        extended = jnp.dot(space_t, window, preferred_element_type=jnp.float32)
        prior_col = jnp.where(block == 0, initial_state, extended[:, 0])
        state = extended[:, 1:]
        earlier = jnp.concatenate([prior_col[:, None], extended[:, 1:-1]], axis=1)
        forcing = lax.dynamic_slice_in_dim(source_padded, begin, STEP_DEV + 1, 1).astype(jnp.float32)
        padded = jnp.pad(state, ((W, W), (0, 0)))
        residual = mass_col * (state - earlier) + diffuse(padded, rates_padded, NODES) + react_col * state * state * state - forcing
        inside = jnp.arange(STEP_DEV, dtype=jnp.int32) + begin + 1 < STEPS
        current = residual[:, :STEP_DEV]
        later = jnp.where(inside[None, :], residual[:, 1:], 0.0)
        present = state[:, :STEP_DEV]
        descent = mass_col * (current - later) + diffuse(jnp.pad(current, ((W, W), (0, 0))), rates_padded, NODES) + 3.0 * react_col * present * present * current
        descent_b = descent.astype(jnp.bfloat16)
        own_steps = lax.dynamic_slice_in_dim(time_factor, begin, STEP_DEV, 1)
        accum = accum + lax.dot_general(own_steps, descent_b, (((1,), (1,)), ((), ())), preferred_element_type=jnp.float32)
        block_grad = jnp.dot(space_factor, descent_b, preferred_element_type=jnp.float32)
        return (accum, block_grad)
    start_sum = jnp.zeros((R, NODES), jnp.float32)
    total, pieces = lax.scan(advance, start_sum, jnp.arange(N_TM, dtype=jnp.int32))
    grad_space = total / math.sqrt(STEPS)
    grad_time = jnp.transpose(pieces, (1, 0, 2)).reshape(R, STEPS) / math.sqrt(NODES)
    return (grad_space, grad_time)
```

```python
import functools
import math

import jax
import jax.numpy as jnp
from jax import lax
from jax.experimental import pallas as pl
from jax.experimental.pallas import tpu as pltpu
from jax.sharding import PartitionSpec as P

W = 4
LANES = 128
CHUNK = 512
LAG = 2
MESH = pl.DeviceIdType.MESH


def from_behind(array, axis, by):
    length = lax.axis_size(axis)
    pairs = [(i, i + by) for i in range(length) if 0 <= i + by < length]
    return lax.ppermute(array, axis, pairs)


def padded_2(array, sides, width):
    for axis, dim in sides:
        size, length = (lax.axis_size(axis), array.shape[dim])
        up = [(i, (i + 1) % size) for i in range(size - 1)]
        down = [(j, i) for i, j in up]
        last = lax.slice_in_dim(array, length - width, length, axis=dim)
        initial = lax.slice_in_dim(array, 0, width, axis=dim)
        before = lax.ppermute(last, axis, up)
        after = lax.ppermute(initial, axis, down)
        array = jnp.concatenate([before, array, after], axis=dim)
    return array


def diffuse(padded, rates_padded, count):
    total = None
    for offset in range(1, W + 1):
        own_rate = rates_padded[offset - 1, W : W + count][:, None]
        came_rate = rates_padded[offset - 1, W - offset : W - offset + count][:, None]
        centre = padded[W : W + count]
        term = own_rate * (centre - padded[W + offset : W + offset + count]) - came_rate * (
            padded[W - offset : W - offset + count] - centre
        )
        total = term if total is None else total + term
    return total


def contract(left, right):
    return lax.dot_general(
        left, right, (((0,), (0,)), ((), ())), preferred_element_type=jnp.float32
    )


def body(space_factor, time_factor, initial_state, link, conductivity, mass, reaction, source):
    node_count = space_factor.shape[1]
    step_count = time_factor.shape[1]
    time_full = lax.all_gather(time_factor, "space", axis=0, tiled=True)
    earlier_row = None
    earlier_row = from_behind(time_full[:, -1], "tm", 1)
    space_full = None
    carried = None
    space_full = lax.all_gather(space_factor, "tm", axis=0, tiled=True)
    state = contract(space_full, time_full)
    carried = contract(space_full, earlier_row)
    leading = lax.axis_index("tm") == 0
    prior_col = jnp.where(leading, initial_state, carried)
    earlier = jnp.concatenate([prior_col[:, None], state[:, :-1]], axis=1)
    offsets = jnp.arange(1, W + 1, dtype=jnp.int32)[:, None]
    rates = jnp.where(link[None, :] == offsets, conductivity[None, :], 0.0)
    below_rates = from_behind(rates[:, node_count - W :], "space", 1)
    rates_padded = jnp.concatenate([below_rates, rates], axis=1)
    padded = padded_2(state, (("space", 0),), W)
    mass_col = mass[:, None]
    react_col = reaction[:, None]
    residual = (
        mass_col * (state - earlier)
        + diffuse(padded, rates_padded, node_count)
        + react_col * state * state * state
        - source.astype(jnp.float32)
    )
    following = from_behind(residual[:, 0], "tm", -1)
    later = jnp.concatenate([residual[:, 1:], following[:, None]], axis=1)
    padded_residual = padded_2(residual, (("space", 0),), W)
    descent = (
        mass_col * (residual - later)
        + diffuse(padded_residual, rates_padded, node_count)
        + 3.0 * react_col * state * state * residual
    )
    descent_b = descent.astype(jnp.bfloat16)
    steps_all = step_count * lax.axis_size("tm")
    nodes_all = node_count * lax.axis_size("space")
    picked = time_full
    grad_space = lax.psum_scatter(
        lax.dot_general(
            picked, descent_b, (((1,), (1,)), ((), ())), preferred_element_type=jnp.float32
        ),
        "tm",
        scatter_dimension=0,
        tiled=True,
    ) / math.sqrt(steps_all)
    picked = space_full
    node_sums = lax.psum_scatter(
        jnp.dot(picked, descent_b, preferred_element_type=jnp.float32),
        "space",
        scatter_dimension=0,
        tiled=True,
    )
    grad_time = node_sums / math.sqrt(nodes_all)
    return (grad_space, grad_time)


def fused_kernel(
    n_space, n_tm, chunk,
    space_ref, time_ref, vec_ref, source_ref,
    grad_space_ref, grad_time_ref,
    src_v, s_all, t_all, t_prev, s_ext, edge_out, edge_in, coef, g1, g23, gedge_out, gedge_in,
    h1, h2, weights, pair, u_send, u_recv, e_send, e_recv,
    part, part_in, zsum, z_in, total,
    src_sem, t_send, t_got, tp_sem, s_send, s_got, edge_send, edge_got,
    gedge_send, gedge_got, u_ss, u_rs, e_ss, e_rs, x_ss, x_rs, z_ss, z_rs,
):
    f32, bf16 = jnp.float32, jnp.bfloat16
    s, m = lax.axis_index("space"), lax.axis_index("tm")
    n_z = n_tm // 2
    z, x = lax.div(m, 2), lax.rem(m, 2)
    nodes, steps = source_ref.shape
    half = nodes // 2
    rows = space_ref.shape[0]
    rank = rows * n_tm
    t_rows = time_ref.shape[0]
    count = nodes // chunk
    wide = chunk + 2 * LANES

    def dev(space, tm):
        return {"space": space, "tm": tm}

    def send(src, dst, ss, rs, space, tm):
        return pltpu.make_async_remote_copy(
            src_ref=src, dst_ref=dst, send_sem=ss, recv_sem=rs,
            device_id=dev(space, tm), device_id_type=MESH,
        )

    load = pltpu.make_async_copy(source_ref, src_v, src_sem)
    load.start()
    edge_in[...] = jnp.zeros_like(edge_in)
    gedge_in[...] = jnp.zeros_like(gedge_in)

    barrier = pltpu.get_barrier_semaphore()

    def greet(space, tm):
        pl.semaphore_signal(barrier, inc=1, device_id=dev(space, tm), device_id_type=MESH)

    for k in range(1, n_space):
        greet(lax.rem(s + k, n_space), m)
    for k in range(1, n_z):
        greet(s, lax.rem(z + k, n_z) * 2 + x)
    greet(s, z * 2 + 1 - x)

    @pl.when(m > 0)
    def _():
        for k in range(n_space):
            greet(k, lax.rem(m + n_tm - 1, n_tm))

    @pl.when(m < n_tm - 1)
    def _():
        for k in range(n_space):
            greet(k, lax.rem(m + 1, n_tm))

    first = space_ref[...].astype(f32)
    s_all[m] = jnp.concatenate([first[:, :half], first[:, half:]], axis=0).astype(bf16)
    t_all[s] = time_ref[...]
    expected = (n_space - 1) + (n_z - 1) + 1
    expected = expected + jnp.where(m > 0, n_space, 0) + jnp.where(m < n_tm - 1, n_space, 0)
    pl.semaphore_wait(barrier, expected)

    def t_copy(k):
        return send(t_all.at[s], t_all.at[s], t_send.at[k], t_got.at[k], lax.rem(s + k, n_space), m)

    def s_copy(k):
        return send(s_all.at[m], s_all.at[m], s_send.at[k], s_got.at[k], s, lax.rem(z + k, n_z) * 2 + x)

    def x_copy(k):
        owner = lax.rem(z + n_z - k, n_z) * 2 + x
        return send(s_all.at[owner], s_all.at[owner], s_send.at[n_z + k], s_got.at[n_z + k], s, z * 2 + 1 - x)

    for k in range(1, n_space):
        t_copy(k).start()
    x_copy(0).start()
    for k in range(1, n_z):
        s_copy(k).start()

    link = vec_ref[0:1, :]
    cond = vec_ref[1:2, :]
    mass = vec_ref[2:3, :LANES + nodes][:, LANES:]
    diag = mass
    for d in range(1, W + 1):
        rate = jnp.where(link == d, cond, 0.0)
        own = rate[:, LANES:]
        came = pltpu.roll(rate, d, 1)[:, LANES:]
        coef[d - 1:d, :] = own
        coef[W + d - 1:W + d, :] = came
        diag = diag + own + came
    coef[8:9, :] = diag
    coef[9:10, :] = mass
    coef[16:17, :] = vec_ref[3:4, LANES:]
    lead = jnp.where(m == 0, 1.0, 0.0)
    coef[17:18, :] = mass * vec_ref[4:5, LANES:] * lead
    coef[18:24, :] = jnp.zeros((6, nodes), f32)
    h1[...] = jnp.zeros_like(h1)
    h2[...] = jnp.zeros_like(h2)

    for k in range(1, n_space):
        t_copy(k).wait()

    t_edge = send(t_all.at[:, :, pl.ds(steps - LANES, LANES)], t_prev, tp_sem.at[0], tp_sem.at[1], s, lax.rem(m + 1, n_tm))

    @pl.when(m < n_tm - 1)
    def _():
        t_edge.start()

    for k in range(1, n_z):
        s_copy(k).wait_recv()
        x_copy(k).start()

    @pl.when(m < n_tm - 1)
    def _():
        t_edge.wait_send()

    @pl.when(m > 0)
    def _():
        t_edge.wait_recv()

    @pl.when(m == 0)
    def _():
        t_prev[...] = jnp.zeros_like(t_prev)

    t_full = t_all[...].reshape(rank, steps)
    tf = t_full.astype(f32)
    prev = t_prev[...].reshape(rank, LANES).astype(f32)
    lane = lax.broadcasted_iota(jnp.int32, (rank, steps), 1)
    prev = pltpu.roll(prev, 1, 1)
    prev = jnp.concatenate([prev] + [jnp.zeros_like(prev)] * (steps // LANES - 1), axis=1)
    minus = -jnp.where(lane == 0, prev, pltpu.roll(tf, 1, 1))
    minus = minus.astype(bf16)
    weights[...] = jnp.concatenate([t_full, t_full, minus, minus], axis=0)
    pair[...] = jnp.concatenate([t_full, minus], axis=0)

    for k in range(1, n_z):
        s_copy(k).wait_send()
    for k in range(n_z):
        x_copy(k).wait()

    for k in range(n_tm):
        block = s_all[k].astype(f32)
        s_ext[k * rows:(k + 1) * rows, LANES:LANES + half] = block[:rows]
        s_ext[k * rows:(k + 1) * rows, LANES + half:LANES + nodes] = block[rows:]

    edge_out[0] = s_ext[:, LANES:2 * LANES].astype(bf16)
    edge_out[1] = s_ext[:, nodes:LANES + nodes].astype(bf16)

    def edge_copies(out, inn, ss, rs):
        down = send(out.at[0], inn.at[0], ss.at[0], rs.at[0], lax.rem(s + n_space - 1, n_space), m)
        up = send(out.at[1], inn.at[1], ss.at[1], rs.at[1], lax.rem(s + 1, n_space), m)
        return down, up

    def edges_start(down, up):
        @pl.when(s > 0)
        def _():
            down.start()

        @pl.when(s < n_space - 1)
        def _():
            up.start()

    def edges_wait(down, up):
        @pl.when(s > 0)
        def _():
            down.wait_send()
            up.wait_recv()

        @pl.when(s < n_space - 1)
        def _():
            up.wait_send()
            down.wait_recv()

    s_edges = edge_copies(edge_out, edge_in, edge_send, edge_got)
    edges_start(*s_edges)
    s_ext[:, 0:LANES] = jnp.zeros((rank, LANES), f32)
    s_ext[:, LANES + nodes:] = jnp.zeros((rank, LANES), f32)

    def banded(field, at):
        out = coef[8:9, pl.ds(at, chunk)] * field[:, LANES:LANES + chunk]
        for d in range(1, W + 1):
            ahead = pltpu.roll(field, wide - d, 1)[:, LANES:LANES + chunk]
            behind = pltpu.roll(field, d, 1)[:, LANES:LANES + chunk]
            out = out - coef[d - 1:d, pl.ds(at, chunk)] * ahead
            out = out - coef[W + d - 1:W + d, pl.ds(at, chunk)] * behind
        return out

    def split(v):
        high = v.astype(bf16)
        return high, (v - high.astype(f32)).astype(bf16)

    def dot_t(a, b):
        return lax.dot_general(a, b, (((0,), (0,)), ((), ())), preferred_element_type=f32)

    def dot_n(a, b):
        return lax.dot_general(a, b, (((1,), (0,)), ((), ())), preferred_element_type=f32)

    def dot_r(a, b):
        return lax.dot_general(a, b, (((1,), (1,)), ((), ())), preferred_element_type=f32)

    load.wait()
    e0 = jnp.where(lax.broadcasted_iota(jnp.int32, (1, steps), 1) == 0, 1.0, 0.0)

    def forward(i, carry):
        c = lax.rem(i + 1, count)
        at = pl.multiple_of(c * chunk, chunk)

        @pl.when(i == count - 2)
        def _():
            edges_wait(*s_edges)
            s_ext[:, 0:LANES] = edge_in[1].astype(f32)
            s_ext[:, LANES + nodes:] = edge_in[0].astype(f32)

        field = s_ext[:, pl.ds(at, wide)]
        mid = field[:, LANES:LANES + chunk]
        mass_c = coef[9:10, pl.ds(at, chunk)]
        a_hi, a_lo = split(banded(field, at))
        b_hi, b_lo = split(mass_c * mid)
        left = jnp.concatenate([a_hi, a_lo, b_hi, b_lo], axis=0)
        s_b = mid.astype(bf16)
        cols = coef[16:24, pl.ds(at, chunk)].T
        lin = dot_t(left, weights[...])
        state = dot_t(s_b, pair[0:rank, :])
        cube = cols[:, 0:1] * state * state
        res = lin + cube * state - src_v[pl.ds(at, chunk), :].astype(f32) - cols[:, 1:2] * e0
        q = (3.0 * cube * res).astype(bf16)
        r_hi, r_lo = split(res)
        big = dot_n(left, r_hi)
        small = dot_n(jnp.concatenate([a_hi, b_hi], axis=0), r_lo)
        h1[...] += big[:rank] + big[rank:2 * rank] + small[:rank] + dot_n(s_b, q)
        h2[...] += big[2 * rank:3 * rank] + big[3 * rank:] + small[rank:]
        g = dot_r(pair[...], r_hi) + dot_r(pair[...], r_lo)
        gq = dot_r(pair[0:rank, :], q)
        g1[:, pl.ds(pl.multiple_of(at + LANES, LANES), chunk)] = g[:rank]
        g23[:, pl.ds(at, chunk)] = mass_c * g[rank:] + gq
        return carry

    lax.fori_loop(0, count, forward, 0)

    gedge_out[0] = g1[:, LANES:2 * LANES]
    gedge_out[1] = g1[:, nodes:LANES + nodes]
    g_edges = edge_copies(gedge_out, gedge_in, gedge_send, gedge_got)
    edges_start(*g_edges)
    g1[:, 0:LANES] = jnp.zeros((rank, LANES), f32)
    g1[:, LANES + nodes:] = jnp.zeros((rank, LANES), f32)

    h2v = h2[...]
    shifted = jnp.where(lane == steps - 1, 0.0, pltpu.roll(h2v, steps - 1, 1))
    share = h1[...] - shifted
    for k in range(n_space):
        u_send[k] = share[k * t_rows:(k + 1) * t_rows]
        e_send[k] = h2v[k * t_rows:(k + 1) * t_rows, :LANES]

    def u_copy(k):
        to = lax.rem(s + k, n_space)
        return send(u_send.at[to], u_recv.at[s], u_ss.at[k], u_rs.at[k], to, m)

    def e_copy(k):
        to = lax.rem(s + k, n_space)
        return send(e_send.at[to], e_recv.at[s], e_ss.at[k], e_rs.at[k], to, lax.rem(m + n_tm - 1, n_tm))

    scale = 1.0 / math.sqrt(steps * n_tm)

    def x_part(c):
        return send(part.at[1 - x, c], part_in.at[c], x_ss.at[c], x_rs.at[c], s, z * 2 + 1 - x)

    def z_part(c, k):
        to = lax.rem(z + k, n_z)
        return send(zsum.at[c, to], z_in.at[c, z], z_ss.at[c, k], z_rs.at[c, k], s, to * 2 + x)

    def combine(c):
        x_part(c).wait_recv()
        both = part[x, c] + part_in[c]
        for k in range(n_z):
            zsum[c, k] = both[k * rows:(k + 1) * rows]
        for k in range(1, n_z):
            z_part(c, k).start()

    def backward(i, carry):
        c = lax.rem(i + 1, count)
        at = pl.multiple_of(c * chunk, chunk)

        @pl.when(i == count - 2)
        def _():
            edges_wait(*g_edges)
            g1[:, 0:LANES] = gedge_in[1]
            g1[:, LANES + nodes:] = gedge_in[0]

        out = (banded(g1[:, pl.ds(at, wide)], at) + g23[:, pl.ds(at, chunk)]) * scale
        for side in range(2):
            part[side, c] = jnp.concatenate(
                [out[(2 * k + side) * rows:(2 * k + side + 1) * rows] for k in range(n_z)], axis=0
            )
        x_part(c).start()

        @pl.when(i >= LAG)
        def _():
            combine(lax.rem(i - LAG + 1 + count, count))

        return carry

    lax.fori_loop(0, count, backward, 0)

    for k in range(1, n_space):
        u_copy(k).start()

    @pl.when(m > 0)
    def _():
        for k in range(n_space):
            e_copy(k).start()

    for i in range(count - LAG, count):
        combine((i + 1) % count)

    for k in range(1, n_space):
        u_copy(k).wait()

    @pl.when(m > 0)
    def _():
        for k in range(n_space):
            e_copy(k).wait_send()

    @pl.when(m < n_tm - 1)
    def _():
        for k in range(n_space):
            e_copy(k).wait_recv()

    @pl.when(m == n_tm - 1)
    def _():
        e_recv[...] = jnp.zeros_like(e_recv)

    mine = u_send[s]
    for k in range(1, n_space):
        mine = mine + u_recv[lax.rem(s + k, n_space)]
    edge = e_recv[0]
    for k in range(1, n_space):
        edge = edge + e_recv[k]
    at_end = lax.broadcasted_iota(jnp.int32, (t_rows, LANES), 1) == LANES - 1
    edge = jnp.where(at_end, pltpu.roll(edge, LANES - 1, 1), 0.0)
    edge = jnp.concatenate([jnp.zeros((t_rows, steps - LANES), f32), edge], axis=1)
    grad_time_ref[...] = (mine - edge) * (1.0 / math.sqrt(nodes * n_space))

    def finish(i, carry):
        c = lax.rem(i + 1, count)
        at = pl.multiple_of(c * chunk, chunk)
        total_c = zsum[c, z]
        for k in range(1, n_z):
            z_part(c, k).wait()
            total_c = total_c + z_in[c, lax.rem(z + n_z - k, n_z)]
        x_part(c).wait_send()
        grad_space_ref[:, pl.ds(at, chunk)] = total_c
        return carry

    lax.fori_loop(0, count, finish, 0)


def fused(n_space, n_tm, space_factor, time_factor, initial_state, link, conductivity, mass, reaction, source):
    f32, bf16 = jnp.float32, jnp.bfloat16
    nodes, steps = source.shape
    rows, t_rows = space_factor.shape[0], time_factor.shape[0]
    rank = rows * n_tm
    chunk = CHUNK
    count = nodes // chunk
    n_z = n_tm // 2
    ends = jnp.stack([link[nodes - LANES:].astype(f32), conductivity[nodes - LANES:]])
    ends = from_behind(ends, "space", 1)
    body = jnp.stack([link.astype(f32), conductivity, mass, reaction, initial_state])
    vec = jnp.concatenate([jnp.pad(ends, ((0, 3), (0, 0))), body], axis=1)
    vec = jnp.pad(vec, ((0, 3), (0, 0)))
    dma, V = pltpu.SemaphoreType.DMA, pltpu.VMEM
    scratch = [
        V((nodes, steps), bf16), V((n_tm, 2 * rows, nodes // 2), bf16),
        V((n_space, t_rows, steps), bf16), V((n_space, t_rows, LANES), bf16),
        V((rank, nodes + 2 * LANES), f32), V((2, rank, LANES), bf16), V((2, rank, LANES), bf16),
        V((24, nodes), f32), V((rank, nodes + 2 * LANES), f32), V((rank, nodes), f32),
        V((2, rank, LANES), f32), V((2, rank, LANES), f32),
        V((rank, steps), f32), V((rank, steps), f32),
        V((4 * rank, steps), bf16), V((2 * rank, steps), bf16),
        V((n_space, t_rows, steps), f32), V((n_space, t_rows, steps), f32),
        V((n_space, t_rows, LANES), f32), V((n_space, t_rows, LANES), f32),
        V((2, count, n_z * rows, chunk), f32), V((count, n_z * rows, chunk), f32),
        V((count, n_z, rows, chunk), f32), V((count, n_z, rows, chunk), f32),
        V((8, LANES), f32),
        dma, dma((n_space,)), dma((n_space,)), dma((2,)), dma((2 * n_z,)), dma((2 * n_z,)),
        dma((2,)), dma((2,)), dma((2,)), dma((2,)),
        dma((n_space,)), dma((n_space,)), dma((n_space,)), dma((n_space,)),
        dma((count,)), dma((count,)), dma((count, n_z)), dma((count, n_z)),
    ]
    vm = pl.BlockSpec(memory_space=pltpu.VMEM)
    return pl.pallas_call(
        functools.partial(fused_kernel, n_space, n_tm, chunk),
        out_shape=(
            jax.ShapeDtypeStruct((rows, nodes), f32),
            jax.ShapeDtypeStruct((t_rows, steps), f32),
        ),
        in_specs=[vm, vm, vm, pl.BlockSpec(memory_space=pl.ANY)],
        out_specs=(vm, vm),
        scratch_shapes=scratch,
        compiler_params=pltpu.CompilerParams(
            collective_id=0, has_side_effects=True, vmem_limit_bytes=48 * 1024 * 1024
        ),
        name="fused",
    )(space_factor, time_factor, vec, source)


def solution(mesh):
    in_specs = (
        P("tm", "space"),
        P("space", "tm"),
        P("space"),
        P("space"),
        P("space"),
        P("space"),
        P("space"),
        P("space", "tm"),
    )
    out_specs = (P("tm", "space"), P("space", "tm"))
    n_space, n_tm = mesh.shape["space"], mesh.shape["tm"]

    def run(space_factor, time_factor, *rest):
        nodes, steps = rest[-1].shape
        fits = (
            space_factor.shape[0] % 8 == 0 and time_factor.shape[0] % 16 == 0 and n_tm % 2 == 0
            and nodes % (2 * CHUNK) == 0 and nodes >= 4 * CHUNK and steps % LANES == 0
        )
        if fits:
            return fused(n_space, n_tm, space_factor, time_factor, *rest)
        return body(space_factor, time_factor, *rest)

    return jax.shard_map(run, mesh=mesh, in_specs=in_specs, out_specs=out_specs, check_vma=False)
```
